1024 devices in a mesh: dp: 128 (over z, x), tensor: 8 (over y, core).
Axes of the slice: x: 4, y: 4, z: 32, core: 2. Of those that a mesh axis runs over, the one named last changes fastest.
Arguments:
- activations: bfloat16 [65536, 8192], P('dp', 'tensor'), may hold values from -6 to 6
- output_gradient: bfloat16 [65536, 1024], P(('dp', 'tensor')), may hold values from -0.25 to 0.25
- momentum: bfloat16 [128, 8192, 1024], P('dp', 'tensor'), may hold values from -6 to 6
Outputs:
- update: bfloat16 [8192, 1024], P('tensor')
The draws below stay inside these ranges and needn't reach their ends.
All inputs are finite; a program needn't handle non-finite values.
Results may differ from the reference program's by a relative error of at most 0.0051.
Values may be sent and summed in bfloat16 or wider, within the bound.
A program may use at most 64 MiB of HBM per device.

```python
import jax
import jax.numpy as jnp
from jax import lax

MODEL_WIDTH = 8192
KEY_VALUE_WIDTH = 1024
REPLICA_TOKENS = 512
BLOCK_SIDE = 64
KEPT_FREQUENCY = 8
REPLICA_COUNT = 128
TOKEN_TOTAL = 65536


def shard_levels(rng, shape, pieces, low, high):
    loudness = 1.0
    for axis_at, blocks in pieces:
        draws = jax.random.uniform(jax.random.fold_in(jax.random.fold_in(rng, 6), axis_at), (blocks,), jnp.float32, low / len(pieces), high / len(pieces))
        loudness = loudness * jnp.repeat(jnp.exp(draws), shape[axis_at] // blocks).reshape((-1,) + (1,) * (len(shape) - 1 - axis_at))
    return loudness


def centred(own_key, shape, deviation, most, split=(), kind=jnp.bfloat16):
    loudness = shard_levels(own_key, shape, split, -0.22, 0.18) if split else 1.0
    values = jax.random.normal(own_key, shape, jnp.float32) * deviation * loudness
    return jnp.minimum(jnp.maximum(values, -most), most).astype(kind)


def setup_inputs(seed: int = 0) -> dict:
    keys = jax.random.split(jax.random.key(seed), 4)
    return {
        "activations": centred(keys[0], (TOKEN_TOTAL, MODEL_WIDTH), 1.0, 6.0, ((0, 128), (1, 8))),
        "output_gradient": centred(keys[1], (TOKEN_TOTAL, KEY_VALUE_WIDTH), REPLICA_TOKENS ** -0.5, 0.25, ((0, 1024),)),
        "momentum": centred(keys[2], (REPLICA_COUNT, MODEL_WIDTH, KEY_VALUE_WIDTH), 1.0, 6.0, ((0, 128), (1, 8))),
    }


def dct_basis():
    freq = jnp.arange(KEPT_FREQUENCY).astype(jnp.float32)[:, None]
    place = jnp.arange(BLOCK_SIDE).astype(jnp.float32)[None, :]
    scales = jnp.where(freq == 0.0, jnp.sqrt(1.0 / BLOCK_SIDE), jnp.sqrt(2.0 / BLOCK_SIDE)).astype(jnp.float32)
    return (scales * jnp.cos(jnp.pi * (2.0 * place + 1.0) * freq / (2.0 * BLOCK_SIDE))).astype(jnp.float32)

def compress(moment, basis):
    row_count, col_count = moment.shape
    blocks = moment.reshape(row_count // BLOCK_SIDE, BLOCK_SIDE, col_count // BLOCK_SIDE, BLOCK_SIDE)
    half = jnp.einsum('ka,iajb->ikjb', basis, blocks, precision=lax.Precision.HIGHEST)
    table = jnp.einsum('ikjb,lb->ikjl', half, basis, precision=lax.Precision.HIGHEST)
    return table.reshape(row_count // BLOCK_SIDE * KEPT_FREQUENCY, col_count // BLOCK_SIDE * KEPT_FREQUENCY)

def expand(table, basis):
    row_blocks = table.shape[0] // KEPT_FREQUENCY
    col_blocks = table.shape[1] // KEPT_FREQUENCY
    coeffs = table.reshape(row_blocks, KEPT_FREQUENCY, col_blocks, KEPT_FREQUENCY)
    half = jnp.einsum('ikjl,lb->ikjb', coeffs, basis, precision=lax.Precision.HIGHEST)
    blocks = jnp.einsum('ka,ikjb->iajb', basis, half, precision=lax.Precision.HIGHEST)
    return blocks.reshape(row_blocks * BLOCK_SIDE, col_blocks * BLOCK_SIDE)

def reference(activations, output_gradient, momentum):
    basis = dct_basis()
    replicas = momentum.shape[0]
    replica_acts = activations.reshape(replicas, -1, activations.shape[1])
    replica_grads = output_gradient.reshape(replicas, -1, output_gradient.shape[1])

    def step(total, item):
        acts_rows, grad_rows, moment_old = item
        gradient = lax.dot_general(acts_rows, grad_rows, (((0,), (0,)), ((), ())), preferred_element_type=jnp.float32)
        moment = 0.9 * moment_old.astype(jnp.float32) + gradient
        coeffs = compress(moment, basis).astype(jnp.bfloat16)
        coeffs = lax.optimization_barrier(coeffs).astype(jnp.float32)
        return (total + coeffs, None)
    zero_filled = jnp.zeros((MODEL_WIDTH // BLOCK_SIDE * KEPT_FREQUENCY, KEY_VALUE_WIDTH // BLOCK_SIDE * KEPT_FREQUENCY), jnp.float32)
    summed, _ = lax.scan(step, zero_filled, (replica_acts, replica_grads, momentum))
    return expand(summed, basis).astype(jnp.bfloat16)
```

```python
import jax
import jax.numpy as jnp
import numpy as np
from jax import lax
from jax.experimental import pallas as pl
from jax.experimental.pallas import tpu as pltpu
from jax.sharding import PartitionSpec as P
import ml_dtypes

BLOCK_SIDE = 64
KEPT_FREQUENCY = 8
MESH = pl.DeviceIdType.MESH
F32 = jnp.float32
BF16 = jnp.bfloat16

ROWS = 1024
COLS = 1024
TOKENS = 512
KEPT = ROWS // BLOCK_SIDE * KEPT_FREQUENCY
TENSOR = 8
SHARE = TOKENS // TENSOR
GROUP = 16
STRIP = KEPT // GROUP
SQUARES = 8


def block_basis():
    freq = np.arange(KEPT_FREQUENCY)[:, None]
    place = np.arange(BLOCK_SIDE)[None, :]
    scales = np.where(freq == 0, np.sqrt(1.0 / BLOCK_SIDE), np.sqrt(2.0 / BLOCK_SIDE))
    basis = scales * np.cos(np.pi * (2.0 * place + 1.0) * freq / (2.0 * BLOCK_SIDE))
    return np.kron(np.eye(ROWS // BLOCK_SIDE), basis).astype(np.float32)


def two_parts(value, axis):
    high = value.astype(BF16)
    low = (value - high.astype(F32)).astype(BF16)
    return jnp.concatenate([high, low], axis=axis)


def fold_rows(value):
    half = value.shape[0] // 2
    return value[:half] + value[half:]


def fold_cols(value):
    half = value.shape[1] // 2
    return value[:, :half] + value[:, half:]


def dot(a, b):
    return jnp.dot(a, b, preferred_element_type=F32)


def dot_nt(a, b):
    return lax.dot_general(a, b, (((1,), (1,)), ((), ())), preferred_element_type=F32)


def reduce_kernel(
    acts_hbm, grad_hbm, moment_hbm, wide_hbm, tall_hbm, out_ref,
    acts, grad, moment, wide_full, tall_full, wide, tall, gathered, coeffs, strips, partials, table,
    load_sem, gather_send, gather_recv, strip_send, strip_recv,
    partial_send, partial_recv, table_send, table_recv, known,
):
    dp, tensor = lax.axis_index("dp"), lax.axis_index("tensor")
    square, place = dp // GROUP, lax.rem(dp, GROUP)

    def peer(step):
        return (dp, lax.rem(tensor + step, TENSOR))

    def mate(step):
        return (square * GROUP + lax.rem(place + step, GROUP), tensor)

    def ahead(step):
        return (lax.rem(square + step, SQUARES) * GROUP + place, tensor)

    barrier = pltpu.get_barrier_semaphore()
    greeted = [ahead(1), ahead(SQUARES - 1)]
    greeted += [mate(step) for step in range(1, GROUP)]
    greeted += [peer(step) for step in range(1, TENSOR)]
    for device in greeted:
        pl.semaphore_signal(barrier, inc=1, device_id=device, device_id_type=MESH)

    loads = [
        pltpu.make_async_copy(source, target, load_sem.at[i])
        for i, (source, target) in enumerate(
            [(grad_hbm, grad), (tall_hbm, tall_full), (wide_hbm, wide_full), (acts_hbm, acts)]
            + [
                (moment_hbm.at[0, pl.ds(256 * i, 256)], moment.at[pl.ds(256 * i, 256)])
                for i in range(4)
            ]
        )
    ]
    for load in loads:
        load.start()

    loads[0].wait()
    loads[1].wait()
    tall[...] = two_parts(tall_full[...], 1)
    mine = pl.ds(pl.multiple_of(tensor * SHARE, SHARE), SHARE)
    gathered[mine] = fold_cols(dot(grad[...], tall[...])).astype(BF16)
    pl.semaphore_wait(barrier, len(greeted))
    gathers = []
    for step in (4, 3, 5, 2, 6, 7, 1):
        copy = pltpu.make_async_remote_copy(
            src_ref=gathered.at[mine],
            dst_ref=gathered.at[mine],
            send_sem=gather_send.at[step],
            recv_sem=gather_recv.at[step],
            device_id=peer(step),
            device_id_type=MESH,
        )
        copy.start()
        gathers.append(copy)

    def pass_on(step, both=True):
        pl.semaphore_signal(known.at[0, step], inc=1, device_id=ahead(1), device_id_type=MESH)
        if both:
            pl.semaphore_signal(
                known.at[1, step], inc=1, device_id=ahead(SQUARES - 1), device_id_type=MESH
            )

    pass_on(0)

    loads[2].wait()
    wide[...] = two_parts(wide_full[...], 0)
    loads[3].wait()
    rows = two_parts(fold_rows(dot_nt(wide[...], acts[...])), 0)
    kept = jnp.zeros((2 * KEPT, 2 * KEPT), F32)
    for i in range(4):
        loads[4 + i].wait()
        part = slice(256 * i, 256 * (i + 1))
        half = two_parts(fold_cols(dot(moment[part], tall[...])), 1)
        kept += dot(wide[:, part], half)
    kept = 0.9 * fold_cols(fold_rows(kept))

    pl.semaphore_wait(known.at[0, 0], 1)
    pl.semaphore_wait(known.at[1, 0], 1)
    pass_on(1)

    for copy in gathers:
        copy.wait_recv()
    found = fold_rows(dot(rows, gathered[...])) + kept
    coeffs[...] = found.reshape(GROUP, STRIP, KEPT)

    sent = []
    for step in (10, 6, 9, 11, 5, 7, 14, 2, 13, 3, 8, 15, 1, 12, 4):
        copy = pltpu.make_async_remote_copy(
            src_ref=coeffs.at[lax.rem(place + step, GROUP)],
            dst_ref=strips.at[step],
            send_sem=strip_send.at[step],
            recv_sem=strip_recv.at[step],
            device_id=mate(step),
            device_id_type=MESH,
        )
        copy.start()
        sent.append(copy)
    pl.semaphore_wait(known.at[0, 1], 1)
    pl.semaphore_wait(known.at[1, 1], 1)
    pass_on(2, both=False)
    strips[0] = coeffs[place]
    for copy in sent:
        copy.wait_recv()
    partials[square] = jnp.sum(strips[...], axis=0)
    pl.semaphore_wait(known.at[0, 2], 1)

    crossed = []
    for step in (4, 3, 5, 2, 6, 1, 7):
        copy = pltpu.make_async_remote_copy(
            src_ref=partials.at[square],
            dst_ref=partials.at[square],
            send_sem=partial_send.at[step],
            recv_sem=partial_recv.at[step],
            device_id=ahead(step),
            device_id_type=MESH,
        )
        copy.start()
        crossed.append(copy)
    for copy in crossed:
        copy.wait_recv()
    table[place] = jnp.sum(partials[...], axis=0)

    spread = []
    for step in (10, 6, 9, 11, 5, 7, 14, 2, 13, 3, 8, 15, 1, 12, 4):
        copy = pltpu.make_async_remote_copy(
            src_ref=table.at[place],
            dst_ref=table.at[place],
            send_sem=table_send.at[step],
            recv_sem=table_recv.at[step],
            device_id=mate(step),
            device_id_type=MESH,
        )
        copy.start()
        spread.append(copy)
    for copy in gathers + sent + crossed:
        copy.wait_send()
    for copy in spread:
        copy.wait_recv()
    out_ref[...] = table[...].reshape(KEPT, KEPT)
    for copy in spread:
        copy.wait_send()


def expand_kernel(summed_ref, wide_ref, block_ref, out_hbm, out, out_sem):
    summed = two_parts(summed_ref[...], 0)
    wide = two_parts(wide_ref[...], 0)
    half = fold_rows(dot(summed, wide[:KEPT])) + dot(summed[:KEPT], wide[KEPT:])
    half = two_parts(half, 0)
    block = block_ref[...].astype(BF16)
    copies = []
    for i in range(4):
        high = half[32 * i : 32 * (i + 1)]
        low = half[KEPT + 32 * i : KEPT + 32 * (i + 1)]
        out[i] = dot(block, jnp.concatenate([high, high, low], axis=0)).astype(BF16)
        copy = pltpu.make_async_copy(out.at[i], out_hbm.at[pl.ds(256 * i, 256)], out_sem.at[i])
        copy.start()
        copies.append(copy)
    for copy in copies:
        copy.wait()


def per_device(activations, output_gradient, momentum):
    wide = block_basis()
    corner = wide[:32, :256].T
    high = corner.astype(ml_dtypes.bfloat16).astype(np.float32)
    block = np.concatenate([high, corner - high, high], axis=1)
    wide, tall, block = jnp.asarray(wide), jnp.asarray(wide.T.copy()), jnp.asarray(block)
    anywhere = pl.BlockSpec(memory_space=pl.ANY)
    in_vmem = pl.BlockSpec(memory_space=pltpu.VMEM)
    dma = pltpu.SemaphoreType.DMA
    summed = pl.pallas_call(
        reduce_kernel,
        out_shape=jax.ShapeDtypeStruct((KEPT, KEPT), F32),
        in_specs=[anywhere] * 5,
        out_specs=in_vmem,
        scratch_shapes=[
            pltpu.VMEM((TOKENS, ROWS), BF16),
            pltpu.VMEM((SHARE, COLS), BF16),
            pltpu.VMEM((ROWS, COLS), BF16),
            pltpu.VMEM((KEPT, ROWS), F32),
            pltpu.VMEM((ROWS, KEPT), F32),
            pltpu.VMEM((2 * KEPT, ROWS), BF16),
            pltpu.VMEM((ROWS, 2 * KEPT), BF16),
            pltpu.VMEM((TOKENS, KEPT), BF16),
            pltpu.VMEM((GROUP, STRIP, KEPT), F32),
            pltpu.VMEM((GROUP, STRIP, KEPT), F32),
            pltpu.VMEM((SQUARES, STRIP, KEPT), F32),
            pltpu.VMEM((GROUP, STRIP, KEPT), F32),
            dma((8,)),
            dma((TENSOR,)),
            dma((TENSOR,)),
            dma((GROUP,)),
            dma((GROUP,)),
            dma((SQUARES,)),
            dma((SQUARES,)),
            dma((GROUP,)),
            dma((GROUP,)),
            pltpu.SemaphoreType.REGULAR((2, 3)),
        ],
        compiler_params=pltpu.CompilerParams(
            collective_id=0, has_side_effects=True, vmem_limit_bytes=60 * 2**20
        ),
        name="reduce",
    )(activations, output_gradient, momentum, wide, tall)
    return pl.pallas_call(
        expand_kernel,
        out_shape=jax.ShapeDtypeStruct((ROWS, COLS), BF16),
        in_specs=[in_vmem] * 3,
        out_specs=anywhere,
        scratch_shapes=[pltpu.VMEM((4, 256, COLS), BF16), dma((4,))],
        compiler_params=pltpu.CompilerParams(vmem_limit_bytes=60 * 2**20),
        name="expand",
    )(summed, wide, block)


def solution(mesh):
    return jax.shard_map(
        per_device,
        mesh=mesh,
        in_specs=(P("dp", "tensor"), P(("dp", "tensor"), None), P("dp", "tensor", None)),
        out_specs=P("tensor", None),
        check_vma=False,
    )
```

```python
import functools

import jax
import jax.numpy as jnp
import numpy as np
from jax import lax
from jax.experimental import pallas as pl
from jax.experimental.pallas import tpu as pltpu
from jax.sharding import PartitionSpec as P
import ml_dtypes

BLOCK_SIDE = 64
KEPT_FREQUENCY = 8
MESH = pl.DeviceIdType.MESH
F32 = jnp.float32
BF16 = jnp.bfloat16

ROWS = 1024
COLS = 1024
TOKENS = 512
KEPT = ROWS // BLOCK_SIDE * KEPT_FREQUENCY
TENSOR = 8
SHARE = TOKENS // TENSOR
GROUP = 16
OWNERS = 8
STRIP = KEPT // OWNERS
SQUARES = 8
FAR = SQUARES // 2
ORDER = (0, 1, 2, 7, 6, 3, 5)
LEVELS = (4, 2)


def block_basis():
    freq = np.arange(KEPT_FREQUENCY)[:, None]
    place = np.arange(BLOCK_SIDE)[None, :]
    scales = np.where(freq == 0, np.sqrt(1.0 / BLOCK_SIDE), np.sqrt(2.0 / BLOCK_SIDE))
    basis = scales * np.cos(np.pi * (2.0 * place + 1.0) * freq / (2.0 * BLOCK_SIDE))
    return np.kron(np.eye(ROWS // BLOCK_SIDE), basis).astype(np.float32)


def two_parts(value, axis):
    high = value.astype(BF16)
    low = (value - high.astype(F32)).astype(BF16)
    return jnp.concatenate([high, low], axis=axis)


def fold_rows(value):
    half = value.shape[0] // 2
    return value[:half] + value[half:]


def fold_cols(value):
    half = value.shape[1] // 2
    return value[:, :half] + value[:, half:]


def dot(a, b):
    return jnp.dot(a, b, preferred_element_type=F32)


def dot_nt(a, b):
    return lax.dot_general(a, b, (((1,), (1,)), ((), ())), preferred_element_type=F32)


def step_kernel(
    acts_hbm, grad_hbm, moment_hbm, wide_hbm, tall_hbm, block_hbm, out_ref,
    acts, grad, moment, wide_full, tall_full, block, wide, tall, gathered, coeffs, strips, partials, table, total,
    load_sem, gather_send, gather_recv, strip_send, strip_recv,
    first_send, across_send, partial_recv, table_send, table_recv, known,
):
    dp, tensor = lax.axis_index("dp"), lax.axis_index("tensor")
    square, place = dp // GROUP, lax.rem(dp, GROUP)

    def peer(step):
        return (dp, lax.rem(tensor + step, TENSOR))

    def mate(step):
        return (square * GROUP + lax.rem(place + step, GROUP), tensor)

    def ahead(step):
        return (lax.rem(square + step, SQUARES) * GROUP + place, tensor)

    barrier = pltpu.get_barrier_semaphore()
    greeted = [ahead(1), ahead(SQUARES - 1)]
    greeted += [mate(step) for step in range(1, GROUP)]
    greeted += [peer(step) for step in range(1, TENSOR)]
    for device in greeted:
        pl.semaphore_signal(barrier, inc=1, device_id=device, device_id_type=MESH)

    loads = [
        pltpu.make_async_copy(source, target, load_sem.at[i])
        for i, (source, target) in enumerate(
            [(grad_hbm, grad), (tall_hbm, tall_full), (wide_hbm, wide_full), (acts_hbm, acts)]
            + [
                (moment_hbm.at[0, pl.ds(256 * i, 256)], moment.at[pl.ds(256 * i, 256)])
                for i in range(4)
            ]
            + [(block_hbm, block)]
        )
    ]
    for load in loads:
        load.start()

    loads[0].wait()
    loads[1].wait()
    tall[...] = two_parts(tall_full[...], 1)
    mine = pl.ds(pl.multiple_of(tensor * SHARE, SHARE), SHARE)
    gathered[mine] = fold_cols(dot(grad[...], tall[...])).astype(BF16)
    pl.semaphore_wait(barrier, len(greeted))
    gathers = []
    for step in (4, 3, 5, 2, 6, 7, 1):
        copy = pltpu.make_async_remote_copy(
            src_ref=gathered.at[mine],
            dst_ref=gathered.at[mine],
            send_sem=gather_send.at[step],
            recv_sem=gather_recv.at[step],
            device_id=peer(step),
            device_id_type=MESH,
        )
        copy.start()
        gathers.append(copy)

    def pass_on(way, level):
        if level > 0:
            pl.semaphore_wait(known.at[way, level - 1], 1)
        if level < LEVELS[way]:
            target = ahead(1) if way == 0 else ahead(SQUARES - 1)
            pl.semaphore_signal(known.at[way, level], inc=1, device_id=target, device_id_type=MESH)

    pass_on(0, 0)
    pass_on(1, 0)

    loads[2].wait()
    wide[...] = two_parts(wide_full[...], 0)
    loads[3].wait()
    rows = two_parts(fold_rows(dot_nt(wide[...], acts[...])), 0)
    kept = jnp.zeros((2 * KEPT, 2 * KEPT), F32)
    for i in range(4):
        loads[4 + i].wait()
        part = slice(256 * i, 256 * (i + 1))
        half = two_parts(fold_cols(dot(moment[part], tall[...])), 1)
        kept += dot(wide[:, part], half)
    kept = 0.9 * fold_cols(fold_rows(kept))

    pass_on(0, 1)
    pass_on(1, 1)

    for copy in gathers:
        copy.wait_recv()
    found = fold_rows(dot(rows, gathered[...])) + kept
    coeffs[...] = found.reshape(OWNERS, STRIP, KEPT).astype(BF16)

    is_owner = place < OWNERS

    def to_owner(turn):
        strip = 4 * (turn % 2) + lax.rem(place + (2, 1, 3, 0)[turn // 2], 4)
        return strip != place, pltpu.make_async_remote_copy(
            src_ref=coeffs.at[strip],
            dst_ref=strips.at[place],
            send_sem=strip_send.at[turn],
            recv_sem=strip_recv.at[place],
            device_id=(square * GROUP + strip, tensor),
            device_id_type=MESH,
        )

    for turn in range(OWNERS):
        other, copy = to_owner(turn)
        pl.when(other)(copy.start)
    pass_on(0, 2)
    pass_on(1, 2)
    pass_on(0, 3)

    def to_first(mate):
        return pltpu.make_async_remote_copy(
            src_ref=partials.at[square, place],
            dst_ref=partials.at[square, place],
            send_sem=first_send.at[mate],
            recv_sem=partial_recv.at[square, place],
            device_id=(mate, tensor),
            device_id_type=MESH,
        )

    def across(step):
        return jnp.logical_or(square != FAR, step != SQUARES - FAR), pltpu.make_async_remote_copy(
            src_ref=partials.at[square, place],
            dst_ref=partials.at[square, place],
            send_sem=across_send.at[step],
            recv_sem=partial_recv.at[square, place],
            device_id=ahead(step),
            device_id_type=MESH,
        )

    def to_mate(turn):
        mate = turn // 4 * 4 + lax.rem(place + (2, 1, 3, 0)[turn % 4], 4)
        return mate != place, pltpu.make_async_remote_copy(
            src_ref=total,
            dst_ref=table.at[place],
            send_sem=table_send.at[turn],
            recv_sem=table_recv.at[place],
            device_id=(square * GROUP + mate, tensor),
            device_id_type=MESH,
        )

    def wait_partial(source, strip):
        piece = partials.at[source, strip]
        pltpu.make_async_copy(piece, piece, partial_recv.at[source, strip]).wait()

    @pl.when(is_owner)
    def _():
        strips[place] = coeffs[place]
        for step in range(1, GROUP):
            source = lax.rem(place + step, GROUP)
            pltpu.make_async_copy(strips.at[source], strips.at[source], strip_recv.at[source]).wait()
        partials[square, place] = jnp.sum(strips[...].astype(F32), axis=0).astype(BF16)

    @pl.when(square == FAR)
    def _():
        pass_on(0, 4)

    @pl.when(jnp.logical_and(square == FAR, is_owner))
    def _():
        for mate in range(GROUP):
            to_first(mate).start()

    @pl.when(is_owner)
    def _():
        for step in (4, 3, 5, 2, 6, 1, 7):
            other, copy = across(step)
            pl.when(other)(copy.start)

    @pl.when(square != FAR)
    def _():
        pass_on(0, 4)

    for copy in gathers:
        copy.wait_send()
    for turn in range(OWNERS):
        other, copy = to_owner(turn)
        pl.when(other)(copy.wait_send)
    loads[8].wait()
    square_basis = block[...].astype(BF16)

    @pl.when(is_owner)
    def _():
        for step in (1, 7, 2, 6, 3, 5, 4):
            source = lax.rem(square + step, SQUARES)
            if step == FAR:
                pl.when(square != 0)(functools.partial(wait_partial, source, place))
            else:
                wait_partial(source, place)
        added = partials[0, place].astype(F32)
        for source in ORDER[1:]:
            added += partials[source, place].astype(F32)
        total[...] = added

        @pl.when(square != 0)
        def _():
            total[...] += partials[FAR, place].astype(F32)

        for turn in range(GROUP):
            other, copy = to_mate(turn)
            pl.when(other)(copy.start)
        pltpu.make_async_copy(total, table.at[place], table_recv.at[place]).start()

    for strip in range(OWNERS):
        pltpu.make_async_copy(total, table.at[strip], table_recv.at[strip]).wait()

    @pl.when(square == 0)
    def _():
        for strip in range(OWNERS):
            wait_partial(FAR, strip)
        table[...] += partials[FAR].astype(F32)

    summed = two_parts(table[...].reshape(KEPT, KEPT), 0)
    half = fold_rows(dot(summed, wide[:KEPT])) + dot(summed[:KEPT], wide[KEPT:])
    half = two_parts(half, 0)
    for i in range(4):
        high = half[32 * i : 32 * (i + 1)]
        low = half[KEPT + 32 * i : KEPT + 32 * (i + 1)]
        out_ref[256 * i : 256 * (i + 1)] = dot(
            square_basis, jnp.concatenate([high, high, low], axis=0)
        ).astype(BF16)

    @pl.when(is_owner)
    def _():
        for step in range(1, SQUARES):
            other, copy = across(step)
            pl.when(other)(copy.wait_send)
        for turn in range(GROUP):
            other, copy = to_mate(turn)
            pl.when(other)(copy.wait_send)

    @pl.when(jnp.logical_and(square == FAR, is_owner))
    def _():
        for mate in range(GROUP):
            to_first(mate).wait_send()


def per_device(activations, output_gradient, momentum):
    wide = block_basis()
    corner = wide[:32, :256].T
    high = corner.astype(ml_dtypes.bfloat16).astype(np.float32)
    block = np.concatenate([high, corner - high, high], axis=1)
    wide, tall, block = jnp.asarray(wide), jnp.asarray(wide.T.copy()), jnp.asarray(block)
    anywhere = pl.BlockSpec(memory_space=pl.ANY)
    in_vmem = pl.BlockSpec(memory_space=pltpu.VMEM)
    dma = pltpu.SemaphoreType.DMA
    operands = (activations, output_gradient, momentum, wide, tall, block)
    return pl.pallas_call(
        step_kernel,
        out_shape=pltpu.VMEM((ROWS, COLS), BF16),
        in_specs=[anywhere] * 6,
        out_specs=in_vmem,
        scratch_shapes=[
            pltpu.VMEM((TOKENS, ROWS), BF16),
            pltpu.VMEM((SHARE, COLS), BF16),
            pltpu.VMEM((ROWS, COLS), BF16),
            pltpu.VMEM((KEPT, ROWS), F32),
            pltpu.VMEM((ROWS, KEPT), F32),
            pltpu.VMEM((256, 96), F32),
            pltpu.VMEM((2 * KEPT, ROWS), BF16),
            pltpu.VMEM((ROWS, 2 * KEPT), BF16),
            pltpu.VMEM((TOKENS, KEPT), BF16),
            pltpu.VMEM((OWNERS, STRIP, KEPT), BF16),
            pltpu.VMEM((GROUP, STRIP, KEPT), BF16),
            pltpu.VMEM((SQUARES, OWNERS, STRIP, KEPT), BF16),
            pltpu.VMEM((OWNERS, STRIP, KEPT), F32),
            pltpu.VMEM((STRIP, KEPT), F32),
            dma((9,)),
            dma((TENSOR,)),
            dma((TENSOR,)),
            dma((OWNERS,)),
            dma((GROUP,)),
            dma((GROUP,)),
            dma((SQUARES,)),
            dma((SQUARES, OWNERS)),
            dma((GROUP,)),
            dma((OWNERS,)),
            pltpu.SemaphoreType.REGULAR((2, 4)),
        ],
        compiler_params=pltpu.CompilerParams(
            collective_id=0, has_side_effects=True, vmem_limit_bytes=24 * 2**20
        ),
        name="step",
    )(*[pltpu.with_memory_space_constraint(value, pltpu.HBM) for value in operands])


def solution(mesh):
    return jax.shard_map(
        per_device,
        mesh=mesh,
        in_specs=(P("dp", "tensor"), P(("dp", "tensor"), None), P("dp", "tensor", None)),
        out_specs=P("tensor", None),
        check_vma=False,
    )
```

```python
import functools

import jax
import jax.numpy as jnp
import numpy as np
from jax import lax
from jax.experimental import pallas as pl
from jax.experimental.pallas import tpu as pltpu
from jax.sharding import PartitionSpec as P
import ml_dtypes

BLOCK_SIDE = 64
KEPT_FREQUENCY = 8
MESH = pl.DeviceIdType.MESH
F32 = jnp.float32
BF16 = jnp.bfloat16

ROWS = 1024
COLS = 1024
TOKENS = 512
KEPT = ROWS // BLOCK_SIDE * KEPT_FREQUENCY
TENSOR = 8
SHARE = TOKENS // TENSOR
GROUP = 16
OWNERS = 8
STRIP = KEPT // OWNERS
SQUARES = 8
FAR = SQUARES // 2
ORDER = (0, 1, 2, 7, 6, 3, 5)
LEVELS = (4, 2)


def block_basis():
    freq = np.arange(KEPT_FREQUENCY)[:, None]
    place = np.arange(BLOCK_SIDE)[None, :]
    scales = np.where(freq == 0, np.sqrt(1.0 / BLOCK_SIDE), np.sqrt(2.0 / BLOCK_SIDE))
    basis = scales * np.cos(np.pi * (2.0 * place + 1.0) * freq / (2.0 * BLOCK_SIDE))
    return np.kron(np.eye(ROWS // BLOCK_SIDE), basis).astype(np.float32)


def two_parts(value, axis):
    high = value.astype(BF16)
    low = (value - high.astype(F32)).astype(BF16)
    return jnp.concatenate([high, low], axis=axis)


def fold_rows(value):
    half = value.shape[0] // 2
    return value[:half] + value[half:]


def fold_cols(value):
    half = value.shape[1] // 2
    return value[:, :half] + value[:, half:]


def dot(a, b):
    return jnp.dot(a, b, preferred_element_type=F32)


def dot_nt(a, b):
    return lax.dot_general(a, b, (((1,), (1,)), ((), ())), preferred_element_type=F32)


def step_kernel(
    acts_hbm, grad_hbm, moment_hbm, wide_hbm, tall_hbm, summed_ref, wide,
    acts, grad, moment, wide_full, tall_full, tall, gathered, coeffs, strips, partials, table, total,
    load_sem, gather_send, gather_recv, strip_send, strip_recv,
    first_send, across_send, partial_recv, table_send, table_recv, known,
):
    dp, tensor = lax.axis_index("dp"), lax.axis_index("tensor")
    square, place = dp // GROUP, lax.rem(dp, GROUP)
    core = lax.rem(tensor, 2)

    is_owner = core == 1
    own_table = place >= OWNERS
    held = jnp.where(own_table, tensor, tensor - 1)
    held_strip = lax.rem(place, OWNERS)

    def peer(step):
        return (dp, lax.rem(tensor + step, TENSOR))

    def mate(step):
        return (square * GROUP + lax.rem(place + step, GROUP), tensor)

    def across_cores(step):
        return (square * GROUP + lax.rem(place + step, GROUP), tensor + 1 - 2 * core)

    def ahead(step):
        return (lax.rem(square + step, SQUARES) * GROUP + place, tensor)

    barrier = pltpu.get_barrier_semaphore()
    greeted = [ahead(1), ahead(SQUARES - 1)]
    greeted += [mate(step) for step in range(1, GROUP)]
    greeted += [across_cores(step) for step in range(1, GROUP)]
    greeted += [peer(step) for step in range(1, TENSOR)]
    for device in greeted:
        pl.semaphore_signal(barrier, inc=1, device_id=device, device_id_type=MESH)

    loads = [
        pltpu.make_async_copy(source, target, load_sem.at[i])
        for i, (source, target) in enumerate(
            [(grad_hbm, grad), (tall_hbm, tall_full), (wide_hbm, wide_full), (acts_hbm, acts)]
            + [
                (moment_hbm.at[0, pl.ds(256 * i, 256)], moment.at[pl.ds(256 * i, 256)])
                for i in range(4)
            ]
        )
    ]
    for load in loads:
        load.start()

    loads[0].wait()
    loads[1].wait()
    tall[...] = two_parts(tall_full[...], 1)
    mine = pl.ds(pl.multiple_of(tensor * SHARE, SHARE), SHARE)
    gathered[mine] = fold_cols(dot(grad[...], tall[...])).astype(BF16)
    pl.semaphore_wait(barrier, len(greeted))
    gathers = []
    for step in (4, 3, 5, 2, 6, 7, 1):
        copy = pltpu.make_async_remote_copy(
            src_ref=gathered.at[mine],
            dst_ref=gathered.at[mine],
            send_sem=gather_send.at[step],
            recv_sem=gather_recv.at[step],
            device_id=peer(step),
            device_id_type=MESH,
        )
        copy.start()
        gathers.append(copy)

    def pass_on(way, level):
        if level > 0:
            pl.semaphore_wait(known.at[way, level - 1], 1)
        if level < LEVELS[way]:
            target = ahead(1) if way == 0 else ahead(SQUARES - 1)
            pl.semaphore_signal(known.at[way, level], inc=1, device_id=target, device_id_type=MESH)

    pass_on(0, 0)
    pass_on(1, 0)

    loads[2].wait()
    wide[...] = two_parts(wide_full[...], 0)
    loads[3].wait()
    rows = two_parts(fold_rows(dot_nt(wide[...], acts[...])), 0)
    kept = jnp.zeros((2 * KEPT, 2 * KEPT), F32)
    for i in range(4):
        loads[4 + i].wait()
        part = slice(256 * i, 256 * (i + 1))
        half = two_parts(fold_cols(dot(moment[part], tall[...])), 1)
        kept += dot(wide[:, part], half)
    kept = 0.9 * fold_cols(fold_rows(kept))

    pass_on(0, 1)
    pass_on(1, 1)

    for copy in gathers:
        copy.wait_recv()
    found = fold_rows(dot(rows, gathered[...])) + kept
    coeffs[...] = found.reshape(OWNERS, STRIP, KEPT).astype(BF16)

    def to_owner(turn):
        strip = 4 * (turn % 2) + lax.rem(place + (2, 1, 3, 0)[turn // 2], 4)
        owner = strip + OWNERS * core
        return jnp.logical_or(core == 0, owner != place), pltpu.make_async_remote_copy(
            src_ref=coeffs.at[strip],
            dst_ref=strips.at[place],
            send_sem=strip_send.at[turn],
            recv_sem=strip_recv.at[place],
            device_id=(square * GROUP + owner, tensor + 1 - core),
            device_id_type=MESH,
        )

    for turn in range(OWNERS):
        other, copy = to_owner(turn)
        pl.when(other)(copy.start)
    pass_on(0, 2)
    pass_on(1, 2)
    pass_on(0, 3)

    def to_first(mate):
        return pltpu.make_async_remote_copy(
            src_ref=partials.at[square, held_strip],
            dst_ref=partials.at[square, held_strip],
            send_sem=first_send.at[mate],
            recv_sem=partial_recv.at[square, held_strip],
            device_id=(mate, held),
            device_id_type=MESH,
        )

    def across(step):
        return jnp.logical_or(square != FAR, step != SQUARES - FAR), pltpu.make_async_remote_copy(
            src_ref=partials.at[square, held_strip],
            dst_ref=partials.at[square, held_strip],
            send_sem=across_send.at[step],
            recv_sem=partial_recv.at[square, held_strip],
            device_id=ahead(step),
            device_id_type=MESH,
        )

    def to_mate(turn):
        mate = turn // 4 * 4 + lax.rem(place + (2, 1, 3, 0)[turn % 4], 4)
        elsewhere = jnp.logical_or(jnp.logical_not(own_table), mate != place)
        return elsewhere, pltpu.make_async_remote_copy(
            src_ref=total,
            dst_ref=table.at[held_strip],
            send_sem=table_send.at[turn],
            recv_sem=table_recv.at[held_strip],
            device_id=(square * GROUP + mate, held),
            device_id_type=MESH,
        )

    def wait_strip(source):
        pltpu.make_async_copy(strips.at[source], strips.at[source], strip_recv.at[source]).wait()

    def wait_partial(source, strip):
        piece = partials.at[source, strip]
        pltpu.make_async_copy(piece, piece, partial_recv.at[source, strip]).wait()

    @pl.when(is_owner)
    def _():
        for step in range(1, GROUP):
            wait_strip(lax.rem(place + step, GROUP))

        @pl.when(own_table)
        def _():
            strips[place] = coeffs[held_strip]

        pl.when(jnp.logical_not(own_table))(functools.partial(wait_strip, place))
        partials[square, held_strip] = jnp.sum(strips[...].astype(F32), axis=0).astype(BF16)

    @pl.when(square == FAR)
    def _():
        pass_on(0, 4)

    @pl.when(jnp.logical_and(square == FAR, is_owner))
    def _():
        for mate in range(GROUP):
            to_first(mate).start()

    @pl.when(is_owner)
    def _():
        for step in (4, 3, 5, 2, 6, 1, 7):
            other, copy = across(step)
            pl.when(other)(copy.start)

    @pl.when(square != FAR)
    def _():
        pass_on(0, 4)

    for copy in gathers:
        copy.wait_send()
    for turn in range(OWNERS):
        other, copy = to_owner(turn)
        pl.when(other)(copy.wait_send)

    @pl.when(is_owner)
    def _():
        for step in (1, 7, 2, 6, 3, 5, 4):
            source = lax.rem(square + step, SQUARES)
            if step == FAR:
                pl.when(square != 0)(functools.partial(wait_partial, source, held_strip))
            else:
                wait_partial(source, held_strip)
        added = partials[0, held_strip].astype(F32)
        for source in ORDER[1:]:
            added += partials[source, held_strip].astype(F32)
        total[...] = added

        @pl.when(square != 0)
        def _():
            total[...] += partials[FAR, held_strip].astype(F32)

        for turn in range(GROUP):
            other, copy = to_mate(turn)
            pl.when(other)(copy.start)

        @pl.when(own_table)
        def _():
            pltpu.make_async_copy(total, table.at[held_strip], table_recv.at[held_strip]).start()

    for strip in range(OWNERS):
        pltpu.make_async_copy(total, table.at[strip], table_recv.at[strip]).wait()

    @pl.when(square == 0)
    def _():
        for strip in range(OWNERS):
            wait_partial(FAR, strip)
        summed_ref[...] = (table[...] + partials[FAR].astype(F32)).reshape(KEPT, KEPT)

    @pl.when(square != 0)
    def _():
        summed_ref[...] = table[...].reshape(KEPT, KEPT)

    @pl.when(is_owner)
    def _():
        for step in range(1, SQUARES):
            other, copy = across(step)
            pl.when(other)(copy.wait_send)
        for turn in range(GROUP):
            other, copy = to_mate(turn)
            pl.when(other)(copy.wait_send)

    @pl.when(jnp.logical_and(square == FAR, is_owner))
    def _():
        for mate in range(GROUP):
            to_first(mate).wait_send()


def expand_kernel(summed_ref, wide, block_ref, out_hbm, out, out_sem):
    summed = two_parts(summed_ref[...], 0)
    half = fold_rows(dot(summed, wide[:KEPT])) + dot(summed[:KEPT], wide[KEPT:])
    half = two_parts(half, 0)
    square_basis = block_ref[...].astype(BF16)
    copies = []
    for i in range(4):
        high = half[32 * i : 32 * (i + 1)]
        low = half[KEPT + 32 * i : KEPT + 32 * (i + 1)]
        out[i] = dot(square_basis, jnp.concatenate([high, high, low], axis=0)).astype(BF16)
        copy = pltpu.make_async_copy(out.at[i], out_hbm.at[pl.ds(256 * i, 256)], out_sem.at[i])
        copy.start()
        copies.append(copy)
    for copy in copies:
        copy.wait()


def per_device(activations, output_gradient, momentum):
    wide = block_basis()
    corner = wide[:32, :256].T
    high = corner.astype(ml_dtypes.bfloat16).astype(np.float32)
    block = np.concatenate([high, corner - high, high], axis=1)
    wide, tall, block = jnp.asarray(wide), jnp.asarray(wide.T.copy()), jnp.asarray(block)
    anywhere = pl.BlockSpec(memory_space=pl.ANY)
    in_vmem = pl.BlockSpec(memory_space=pltpu.VMEM)
    dma = pltpu.SemaphoreType.DMA
    operands = (activations, output_gradient, momentum, wide, tall)
    summed, wide = pl.pallas_call(
        step_kernel,
        out_shape=(pltpu.VMEM((KEPT, KEPT), F32), pltpu.VMEM((2 * KEPT, ROWS), BF16)),
        in_specs=[anywhere] * 5,
        out_specs=(in_vmem, in_vmem),
        scratch_shapes=[
            pltpu.VMEM((TOKENS, ROWS), BF16),
            pltpu.VMEM((SHARE, COLS), BF16),
            pltpu.VMEM((ROWS, COLS), BF16),
            pltpu.VMEM((KEPT, ROWS), F32),
            pltpu.VMEM((ROWS, KEPT), F32),
            pltpu.VMEM((ROWS, 2 * KEPT), BF16),
            pltpu.VMEM((TOKENS, KEPT), BF16),
            pltpu.VMEM((OWNERS, STRIP, KEPT), BF16),
            pltpu.VMEM((GROUP, STRIP, KEPT), BF16),
            pltpu.VMEM((SQUARES, OWNERS, STRIP, KEPT), BF16),
            pltpu.VMEM((OWNERS, STRIP, KEPT), F32),
            pltpu.VMEM((STRIP, KEPT), F32),
            dma((8,)),
            dma((TENSOR,)),
            dma((TENSOR,)),
            dma((OWNERS,)),
            dma((GROUP,)),
            dma((GROUP,)),
            dma((SQUARES,)),
            dma((SQUARES, OWNERS)),
            dma((GROUP,)),
            dma((OWNERS,)),
            pltpu.SemaphoreType.REGULAR((2, 4)),
        ],
        compiler_params=pltpu.CompilerParams(
            collective_id=0, has_side_effects=True, vmem_limit_bytes=24 * 2**20
        ),
        name="step",
    )(*[pltpu.with_memory_space_constraint(value, pltpu.HBM) for value in operands])
    return pl.pallas_call(
        expand_kernel,
        out_shape=jax.ShapeDtypeStruct((ROWS, COLS), BF16),
        in_specs=[in_vmem] * 3,
        out_specs=anywhere,
        scratch_shapes=[pltpu.VMEM((4, 256, COLS), BF16), dma((4,))],
        compiler_params=pltpu.CompilerParams(vmem_limit_bytes=24 * 2**20),
        name="expand",
    )(summed, wide, block)


def solution(mesh):
    return jax.shard_map(
        per_device,
        mesh=mesh,
        in_specs=(P("dp", "tensor"), P(("dp", "tensor"), None), P("dp", "tensor", None)),
        out_specs=P("tensor", None),
        check_vma=False,
    )
```

```python
import functools

import jax
import jax.numpy as jnp
import numpy as np
from jax import lax
from jax.experimental import pallas as pl
from jax.experimental.pallas import tpu as pltpu
from jax.sharding import PartitionSpec as P
import ml_dtypes

BLOCK_SIDE = 64
KEPT_FREQUENCY = 8
MESH = pl.DeviceIdType.MESH
F32 = jnp.float32
BF16 = jnp.bfloat16

ROWS = 1024
COLS = 1024
TOKENS = 512
KEPT = ROWS // BLOCK_SIDE * KEPT_FREQUENCY
TENSOR = 8
SHARE = TOKENS // TENSOR
GROUP = 16
OWNERS = 8
STRIP = KEPT // OWNERS
SQUARES = 8
FAR = SQUARES // 2
ORDER = (0, 1, 2, 7, 6)
LAST = (3, 5, FAR)
LEVELS = (4, 3)


def block_basis():
    freq = np.arange(KEPT_FREQUENCY)[:, None]
    place = np.arange(BLOCK_SIDE)[None, :]
    scales = np.where(freq == 0, np.sqrt(1.0 / BLOCK_SIDE), np.sqrt(2.0 / BLOCK_SIDE))
    basis = scales * np.cos(np.pi * (2.0 * place + 1.0) * freq / (2.0 * BLOCK_SIDE))
    return np.kron(np.eye(ROWS // BLOCK_SIDE), basis).astype(np.float32)


def two_parts(value, axis):
    high = value.astype(BF16)
    low = (value - high.astype(F32)).astype(BF16)
    return jnp.concatenate([high, low], axis=axis)


def fold_rows(value):
    half = value.shape[0] // 2
    return value[:half] + value[half:]


def fold_cols(value):
    half = value.shape[1] // 2
    return value[:, :half] + value[:, half:]


def dot(a, b):
    return jnp.dot(a, b, preferred_element_type=F32)


def dot_nt(a, b):
    return lax.dot_general(a, b, (((1,), (1,)), ((), ())), preferred_element_type=F32)


def step_kernel(
    acts_hbm, grad_hbm, moment_hbm, wide_hbm, tall_hbm, summed_ref, wide,
    acts, grad, moment, wide_full, tall_full, tall, rows, gathered, coeffs, strips, partials, table, total,
    load_sem, gather_send, gather_recv, strip_send, strip_recv,
    first_send, across_send, partial_recv, table_send, table_recv, known,
):
    dp, tensor = lax.axis_index("dp"), lax.axis_index("tensor")
    square, place = dp // GROUP, lax.rem(dp, GROUP)
    core = lax.rem(tensor, 2)
    is_far = jnp.logical_and(square >= FAR - 1, square <= FAR + 1)

    is_owner = core == 1
    own_table = place >= OWNERS
    held = jnp.where(own_table, tensor, tensor - 1)
    held_strip = lax.rem(place, OWNERS)

    def peer(step):
        return (dp, lax.rem(tensor + step, TENSOR))

    def mate(step):
        return (square * GROUP + lax.rem(place + step, GROUP), tensor)

    def across_cores(step):
        return (square * GROUP + lax.rem(place + step, GROUP), tensor + 1 - 2 * core)

    def ahead(step):
        return (lax.rem(square + step, SQUARES) * GROUP + place, tensor)

    barrier = pltpu.get_barrier_semaphore()
    greeted = [ahead(1), ahead(SQUARES - 1)]
    greeted += [mate(step) for step in range(1, GROUP)]
    greeted += [across_cores(step) for step in range(1, GROUP)]
    greeted += [peer(step) for step in range(1, TENSOR)]
    for device in greeted:
        pl.semaphore_signal(barrier, inc=1, device_id=device, device_id_type=MESH)

    loads = [
        pltpu.make_async_copy(source, target, load_sem.at[i])
        for i, (source, target) in enumerate(
            [(grad_hbm, grad), (tall_hbm, tall_full), (wide_hbm, wide_full), (acts_hbm, acts)]
            + [
                (moment_hbm.at[0, pl.ds(256 * i, 256)], moment.at[pl.ds(256 * i, 256)])
                for i in range(4)
            ]
        )
    ]
    for load in loads:
        load.start()

    loads[0].wait()
    loads[1].wait()
    tall[...] = two_parts(tall_full[...], 1)
    mine = pl.ds(pl.multiple_of(tensor * SHARE, SHARE), SHARE)
    gathered[mine] = fold_cols(dot(grad[...], tall[...])).astype(BF16)
    pl.semaphore_wait(barrier, len(greeted))
    gathers = []
    for step in (4, 5 - 2 * core, 3 + 2 * core, 2, 6, 7, 1):
        copy = pltpu.make_async_remote_copy(
            src_ref=gathered.at[mine],
            dst_ref=gathered.at[mine],
            send_sem=gather_send.at[step],
            recv_sem=gather_recv.at[step],
            device_id=peer(step),
            device_id_type=MESH,
        )
        copy.start()
        gathers.append(copy)

    def pass_on(way, level):
        if level > 0:
            pl.semaphore_wait(known.at[way, level - 1], 1)
        if level < LEVELS[way]:
            target = ahead(1) if way == 0 else ahead(SQUARES - 1)
            pl.semaphore_signal(known.at[way, level], inc=1, device_id=target, device_id_type=MESH)

    pass_on(0, 0)
    pass_on(1, 0)

    loads[2].wait()
    wide[...] = two_parts(wide_full[...], 0)
    loads[3].wait()
    rows[...] = two_parts(fold_rows(dot_nt(wide[...], acts[...])), 0)
    kept = jnp.zeros((2 * KEPT, 2 * KEPT), F32)
    for i in range(4):
        loads[4 + i].wait()
        part = slice(256 * i, 256 * (i + 1))
        half = two_parts(fold_cols(dot(moment[part], tall[...])), 1)
        kept += dot(wide[:, part], half)
    kept = 0.9 * fold_cols(fold_rows(kept))

    pass_on(0, 1)
    pass_on(1, 1)

    def of_chip(step):
        spot = lax.rem(tensor // 2 + step, TENSOR // 2) * 2 * SHARE
        tokens = pl.ds(pl.multiple_of(spot, 2 * SHARE), 2 * SHARE)
        return dot(rows[:, tokens], gathered[tokens])

    def wait_tokens(step):
        pltpu.make_async_copy(gathered.at[mine], gathered.at[mine], gather_recv.at[step]).wait()

    for step in (1, 2, 6, 7, 5 - 2 * core):
        wait_tokens(step)
    found = of_chip(0) + of_chip(1) + of_chip(3)
    for step in (4, 3 + 2 * core):
        wait_tokens(step)
    found = fold_rows(found + of_chip(2)) + kept
    coeffs[...] = found.reshape(OWNERS, STRIP, KEPT).astype(BF16)

    def to_owner(turn):
        strip = 4 * (turn % 2) + lax.rem(place + (2, 1, 3, 0)[turn // 2], 4)
        owner = strip + OWNERS * core
        return jnp.logical_or(core == 0, owner != place), pltpu.make_async_remote_copy(
            src_ref=coeffs.at[strip],
            dst_ref=strips.at[place],
            send_sem=strip_send.at[turn],
            recv_sem=strip_recv.at[place],
            device_id=(square * GROUP + owner, tensor + 1 - core),
            device_id_type=MESH,
        )

    for turn in range(OWNERS):
        other, copy = to_owner(turn)
        pl.when(other)(copy.start)
    pass_on(0, 2)
    pass_on(1, 2)
    pass_on(0, 3)

    def to_first(mate):
        return pltpu.make_async_remote_copy(
            src_ref=partials.at[square, held_strip],
            dst_ref=partials.at[square, held_strip],
            send_sem=first_send.at[mate],
            recv_sem=partial_recv.at[square, held_strip],
            device_id=(mate, held),
            device_id_type=MESH,
        )

    def across(step):
        return jnp.logical_or(jnp.logical_not(is_far), square + step != SQUARES), pltpu.make_async_remote_copy(
            src_ref=partials.at[square, held_strip],
            dst_ref=partials.at[square, held_strip],
            send_sem=across_send.at[step],
            recv_sem=partial_recv.at[square, held_strip],
            device_id=ahead(step),
            device_id_type=MESH,
        )

    def to_mate(turn):
        mate = turn // 4 * 4 + lax.rem(place + (2, 1, 3, 0)[turn % 4], 4)
        elsewhere = jnp.logical_or(jnp.logical_not(own_table), mate != place)
        return elsewhere, pltpu.make_async_remote_copy(
            src_ref=total,
            dst_ref=table.at[held_strip],
            send_sem=table_send.at[turn],
            recv_sem=table_recv.at[held_strip],
            device_id=(square * GROUP + mate, held),
            device_id_type=MESH,
        )

    def wait_strip(source):
        pltpu.make_async_copy(strips.at[source], strips.at[source], strip_recv.at[source]).wait()

    def wait_partial(source, strip):
        piece = partials.at[source, strip]
        pltpu.make_async_copy(piece, piece, partial_recv.at[source, strip]).wait()

    @pl.when(is_owner)
    def _():
        for step in range(1, GROUP):
            wait_strip(lax.rem(place + step, GROUP))

        @pl.when(own_table)
        def _():
            strips[place] = coeffs[held_strip]

        pl.when(jnp.logical_not(own_table))(functools.partial(wait_strip, place))
        partials[square, held_strip] = jnp.sum(strips[...].astype(F32), axis=0).astype(BF16)

    @pl.when(square == FAR)
    def _():
        pass_on(0, 4)

    @pl.when(square == FAR + 1)
    def _():
        pass_on(1, 3)

    @pl.when(jnp.logical_and(is_far, is_owner))
    def _():
        for mate in range(GROUP):
            to_first(mate).start()

    @pl.when(is_owner)
    def _():
        for step in (4, 3, 5, 2, 6, 1, 7):
            other, copy = across(step)
            pl.when(other)(copy.start)

    @pl.when(square != FAR)
    def _():
        pass_on(0, 4)

    @pl.when(square != FAR + 1)
    def _():
        pass_on(1, 3)

    for copy in gathers:
        copy.wait_send()
    for turn in range(OWNERS):
        other, copy = to_owner(turn)
        pl.when(other)(copy.wait_send)

    @pl.when(is_owner)
    def _():
        for step in (1, 7, 2, 6, 3, 5, 4):
            source = lax.rem(square + step, SQUARES)
            if step in LAST:
                pl.when(square != 0)(functools.partial(wait_partial, source, held_strip))
            else:
                wait_partial(source, held_strip)
        added = partials[0, held_strip].astype(F32)
        for source in ORDER[1:]:
            added += partials[source, held_strip].astype(F32)
        total[...] = added

        @pl.when(square != 0)
        def _():
            added = total[...]
            for source in LAST:
                added += partials[source, held_strip].astype(F32)
            total[...] = added

        for turn in range(GROUP):
            other, copy = to_mate(turn)
            pl.when(other)(copy.start)

        @pl.when(own_table)
        def _():
            pltpu.make_async_copy(total, table.at[held_strip], table_recv.at[held_strip]).start()

    for strip in range(OWNERS):
        pltpu.make_async_copy(total, table.at[strip], table_recv.at[strip]).wait()

    @pl.when(square == 0)
    def _():
        added = table[...]
        for source in LAST:
            for strip in range(OWNERS):
                wait_partial(source, strip)
            added += partials[source].astype(F32)
        summed_ref[...] = added.reshape(KEPT, KEPT)

    @pl.when(square != 0)
    def _():
        summed_ref[...] = table[...].reshape(KEPT, KEPT)

    @pl.when(is_owner)
    def _():
        for step in range(1, SQUARES):
            other, copy = across(step)
            pl.when(other)(copy.wait_send)
        for turn in range(GROUP):
            other, copy = to_mate(turn)
            pl.when(other)(copy.wait_send)

    @pl.when(jnp.logical_and(is_far, is_owner))
    def _():
        for mate in range(GROUP):
            to_first(mate).wait_send()


def expand_kernel(summed_ref, wide, block_ref, out_hbm, out, out_sem):
    summed = two_parts(summed_ref[...], 0)
    half = fold_rows(dot(summed, wide[:KEPT])) + dot(summed[:KEPT], wide[KEPT:])
    half = two_parts(half, 0)
    square_basis = block_ref[...].astype(BF16)
    copies = []
    for i in range(4):
        high = half[32 * i : 32 * (i + 1)]
        low = half[KEPT + 32 * i : KEPT + 32 * (i + 1)]
        out[i] = dot(square_basis, jnp.concatenate([high, high, low], axis=0)).astype(BF16)
        copy = pltpu.make_async_copy(out.at[i], out_hbm.at[pl.ds(256 * i, 256)], out_sem.at[i])
        copy.start()
        copies.append(copy)
    for copy in copies:
        copy.wait()


def per_device(activations, output_gradient, momentum):
    wide = block_basis()
    corner = wide[:32, :256].T
    high = corner.astype(ml_dtypes.bfloat16).astype(np.float32)
    block = np.concatenate([high, corner - high, high], axis=1)
    wide, tall, block = jnp.asarray(wide), jnp.asarray(wide.T.copy()), jnp.asarray(block)
    anywhere = pl.BlockSpec(memory_space=pl.ANY)
    in_vmem = pl.BlockSpec(memory_space=pltpu.VMEM)
    dma = pltpu.SemaphoreType.DMA
    operands = (activations, output_gradient, momentum, wide, tall)
    summed, wide = pl.pallas_call(
        step_kernel,
        out_shape=(pltpu.VMEM((KEPT, KEPT), F32), pltpu.VMEM((2 * KEPT, ROWS), BF16)),
        in_specs=[anywhere] * 5,
        out_specs=(in_vmem, in_vmem),
        scratch_shapes=[
            pltpu.VMEM((TOKENS, ROWS), BF16),
            pltpu.VMEM((SHARE, COLS), BF16),
            pltpu.VMEM((ROWS, COLS), BF16),
            pltpu.VMEM((KEPT, ROWS), F32),
            pltpu.VMEM((ROWS, KEPT), F32),
            pltpu.VMEM((ROWS, 2 * KEPT), BF16),
            pltpu.VMEM((2 * KEPT, TOKENS), BF16),
            pltpu.VMEM((TOKENS, KEPT), BF16),
            pltpu.VMEM((OWNERS, STRIP, KEPT), BF16),
            pltpu.VMEM((GROUP, STRIP, KEPT), BF16),
            pltpu.VMEM((SQUARES, OWNERS, STRIP, KEPT), BF16),
            pltpu.VMEM((OWNERS, STRIP, KEPT), F32),
            pltpu.VMEM((STRIP, KEPT), F32),
            dma((8,)),
            dma((TENSOR,)),
            dma((TENSOR,)),
            dma((OWNERS,)),
            dma((GROUP,)),
            dma((GROUP,)),
            dma((SQUARES,)),
            dma((SQUARES, OWNERS)),
            dma((GROUP,)),
            dma((OWNERS,)),
            pltpu.SemaphoreType.REGULAR((2, 4)),
        ],
        compiler_params=pltpu.CompilerParams(
            collective_id=0, has_side_effects=True, vmem_limit_bytes=24 * 2**20
        ),
        name="step",
    )(*[pltpu.with_memory_space_constraint(value, pltpu.HBM) for value in operands])
    return pl.pallas_call(
        expand_kernel,
        out_shape=jax.ShapeDtypeStruct((ROWS, COLS), BF16),
        in_specs=[in_vmem] * 3,
        out_specs=anywhere,
        scratch_shapes=[pltpu.VMEM((4, 256, COLS), BF16), dma((4,))],
        compiler_params=pltpu.CompilerParams(vmem_limit_bytes=24 * 2**20),
        name="expand",
    )(summed, wide, block)


def solution(mesh):
    return jax.shard_map(
        per_device,
        mesh=mesh,
        in_specs=(P("dp", "tensor"), P(("dp", "tensor"), None), P("dp", "tensor", None)),
        out_specs=P("tensor", None),
        check_vma=False,
    )
```

```python
import functools

import jax
import jax.numpy as jnp
import numpy as np
from jax import lax
from jax.experimental import pallas as pl
from jax.experimental.pallas import tpu as pltpu
from jax.sharding import PartitionSpec as P
import ml_dtypes

BLOCK_SIDE = 64
KEPT_FREQUENCY = 8
MESH = pl.DeviceIdType.MESH
F32 = jnp.float32
BF16 = jnp.bfloat16

ROWS = 1024
COLS = 1024
TOKENS = 512
KEPT = ROWS // BLOCK_SIDE * KEPT_FREQUENCY
TENSOR = 8
SHARE = TOKENS // TENSOR
GROUP = 16
OWNERS = 8
STRIP = KEPT // OWNERS
SQUARES = 8
FAR = SQUARES // 2
ORDER = (0, 1, 2, 7, 6)
LAST = (3, 5, FAR)
LEVELS = (3, 3)


def block_basis():
    freq = np.arange(KEPT_FREQUENCY)[:, None]
    place = np.arange(BLOCK_SIDE)[None, :]
    scales = np.where(freq == 0, np.sqrt(1.0 / BLOCK_SIDE), np.sqrt(2.0 / BLOCK_SIDE))
    basis = scales * np.cos(np.pi * (2.0 * place + 1.0) * freq / (2.0 * BLOCK_SIDE))
    return np.kron(np.eye(ROWS // BLOCK_SIDE), basis).astype(np.float32)


def two_parts(value, axis):
    high = value.astype(BF16)
    low = (value - high.astype(F32)).astype(BF16)
    return jnp.concatenate([high, low], axis=axis)


def fold_rows(value):
    half = value.shape[0] // 2
    return value[:half] + value[half:]


def fold_cols(value):
    half = value.shape[1] // 2
    return value[:, :half] + value[:, half:]


def dot(a, b):
    return jnp.dot(a, b, preferred_element_type=F32)


def dot_nt(a, b):
    return lax.dot_general(a, b, (((1,), (1,)), ((), ())), preferred_element_type=F32)


def step_kernel(
    acts_hbm, grad_hbm, moment_hbm, wide_hbm, tall_hbm, summed_ref, wide,
    acts, grad, moment, wide_full, tall_full, tall, rows, gathered, coeffs, strips, partials, table, total,
    load_sem, gather_send, gather_recv, strip_send, strip_recv,
    first_send, across_send, partial_recv, table_send, table_recv, known,
):
    dp, tensor = lax.axis_index("dp"), lax.axis_index("tensor")
    square, place = dp // GROUP, lax.rem(dp, GROUP)
    core = lax.rem(tensor, 2)
    is_far = jnp.logical_and(square >= FAR - 1, square <= FAR + 1)

    is_owner = core == 1
    own_table = place >= OWNERS
    held = jnp.where(own_table, tensor, tensor - 1)
    held_strip = lax.rem(place, OWNERS)

    def peer(step):
        return (dp, lax.rem(tensor + step, TENSOR))

    def mate(step):
        return (square * GROUP + lax.rem(place + step, GROUP), tensor)

    def across_cores(step):
        return (square * GROUP + lax.rem(place + step, GROUP), tensor + 1 - 2 * core)

    def ahead(step):
        return (lax.rem(square + step, SQUARES) * GROUP + place, tensor)

    barrier = pltpu.get_barrier_semaphore()
    greeted = [ahead(1), ahead(SQUARES - 1)]
    greeted += [mate(step) for step in range(1, GROUP)]
    greeted += [across_cores(step) for step in range(1, GROUP)]
    greeted += [peer(step) for step in range(1, TENSOR)]
    for device in greeted:
        pl.semaphore_signal(barrier, inc=1, device_id=device, device_id_type=MESH)

    @pl.when(square == 0)
    def _():
        for step in range(GROUP):
            spot = GROUP + lax.rem(place + step, GROUP)
            for other in (tensor, tensor + 1 - 2 * core)[1 if step == 0 else 0 :]:
                pl.semaphore_signal(
                    barrier, inc=1, device_id=(spot, other), device_id_type=MESH
                )

    loads = [
        pltpu.make_async_copy(source, target, load_sem.at[i])
        for i, (source, target) in enumerate(
            [(grad_hbm, grad), (tall_hbm, tall_full), (wide_hbm, wide_full), (acts_hbm, acts)]
            + [
                (moment_hbm.at[0, pl.ds(256 * i, 256)], moment.at[pl.ds(256 * i, 256)])
                for i in range(4)
            ]
        )
    ]
    for load in loads:
        load.start()

    loads[0].wait()
    loads[1].wait()
    tall[...] = two_parts(tall_full[...], 1)
    mine = pl.ds(pl.multiple_of(tensor * SHARE, SHARE), SHARE)
    gathered[mine] = fold_cols(dot(grad[...], tall[...])).astype(BF16)
    pl.semaphore_wait(barrier, len(greeted) + jnp.where(square == 1, 2 * GROUP - 1, 0))
    gathers = []
    for step in (4, 5 - 2 * core, 3 + 2 * core, 2, 6, 7, 1):
        copy = pltpu.make_async_remote_copy(
            src_ref=gathered.at[mine],
            dst_ref=gathered.at[mine],
            send_sem=gather_send.at[step],
            recv_sem=gather_recv.at[step],
            device_id=peer(step),
            device_id_type=MESH,
        )
        copy.start()
        gathers.append(copy)

    def pass_on(way, level):
        if level > 0:
            pl.semaphore_wait(known.at[way, level - 1], 1)
        if level < LEVELS[way]:
            target = ahead(1) if way == 0 else ahead(SQUARES - 1)
            pl.semaphore_signal(known.at[way, level], inc=1, device_id=target, device_id_type=MESH)

    pass_on(0, 0)
    pass_on(1, 0)

    loads[2].wait()
    wide[...] = two_parts(wide_full[...], 0)
    loads[3].wait()
    rows[...] = two_parts(fold_rows(dot_nt(wide[...], acts[...])), 0)
    kept = jnp.zeros((2 * KEPT, 2 * KEPT), F32)
    for i in range(4):
        loads[4 + i].wait()
        part = slice(256 * i, 256 * (i + 1))
        half = two_parts(fold_cols(dot(moment[part], tall[...])), 1)
        kept += dot(wide[:, part], half)
    kept = 0.9 * fold_cols(fold_rows(kept))

    pass_on(0, 1)
    pass_on(1, 1)

    def of_chip(step):
        spot = lax.rem(tensor // 2 + step, TENSOR // 2) * 2 * SHARE
        tokens = pl.ds(pl.multiple_of(spot, 2 * SHARE), 2 * SHARE)
        return dot(rows[:, tokens], gathered[tokens])

    def wait_tokens(step):
        pltpu.make_async_copy(gathered.at[mine], gathered.at[mine], gather_recv.at[step]).wait()

    for step in (1, 2, 6, 7, 5 - 2 * core):
        wait_tokens(step)
    found = of_chip(0) + of_chip(1) + of_chip(3)
    for step in (4, 3 + 2 * core):
        wait_tokens(step)
    found = fold_rows(found + of_chip(2)) + kept
    coeffs[...] = found.reshape(OWNERS, STRIP, KEPT).astype(BF16)

    def to_owner(turn):
        strip = 4 * (turn % 2) + lax.rem(place + (2, 1, 3, 0)[turn // 2], 4)
        owner = strip + OWNERS * core
        return jnp.logical_or(core == 0, owner != place), pltpu.make_async_remote_copy(
            src_ref=coeffs.at[strip],
            dst_ref=strips.at[place],
            send_sem=strip_send.at[turn],
            recv_sem=strip_recv.at[place],
            device_id=(square * GROUP + owner, tensor + 1 - core),
            device_id_type=MESH,
        )

    for turn in range(OWNERS):
        other, copy = to_owner(turn)
        pl.when(other)(copy.start)
    pass_on(0, 2)
    pass_on(1, 2)
    pass_on(0, 3)

    def to_first(mate):
        return pltpu.make_async_remote_copy(
            src_ref=partials.at[square, held_strip],
            dst_ref=partials.at[square, held_strip],
            send_sem=first_send.at[mate],
            recv_sem=partial_recv.at[square, held_strip],
            device_id=(mate, held),
            device_id_type=MESH,
        )

    def across(step):
        return jnp.logical_or(jnp.logical_not(is_far), square + step != SQUARES), pltpu.make_async_remote_copy(
            src_ref=partials.at[square, held_strip],
            dst_ref=partials.at[square, held_strip],
            send_sem=across_send.at[step],
            recv_sem=partial_recv.at[square, held_strip],
            device_id=ahead(step),
            device_id_type=MESH,
        )

    def to_mate(turn):
        mate = turn // 4 * 4 + lax.rem(place + (2, 1, 3, 0)[turn % 4], 4)
        elsewhere = jnp.logical_or(jnp.logical_not(own_table), mate != place)
        return elsewhere, pltpu.make_async_remote_copy(
            src_ref=total,
            dst_ref=table.at[held_strip],
            send_sem=table_send.at[turn],
            recv_sem=table_recv.at[held_strip],
            device_id=(square * GROUP + mate, held),
            device_id_type=MESH,
        )

    def wait_strip(source):
        pltpu.make_async_copy(strips.at[source], strips.at[source], strip_recv.at[source]).wait()

    def wait_partial(source, strip):
        piece = partials.at[source, strip]
        pltpu.make_async_copy(piece, piece, partial_recv.at[source, strip]).wait()

    @pl.when(is_owner)
    def _():
        for step in range(1, GROUP):
            wait_strip(lax.rem(place + step, GROUP))

        @pl.when(own_table)
        def _():
            strips[place] = coeffs[held_strip]

        pl.when(jnp.logical_not(own_table))(functools.partial(wait_strip, place))
        partials[square, held_strip] = jnp.sum(strips[...].astype(F32), axis=0).astype(BF16)

    @pl.when(square == FAR + 1)
    def _():
        pass_on(1, 3)

    @pl.when(jnp.logical_and(is_far, is_owner))
    def _():
        for mate in range(GROUP):
            to_first(mate).start()

    @pl.when(is_owner)
    def _():
        for step in (4, 3, 5, 2, 6, 1, 7):
            other, copy = across(step)
            pl.when(other)(copy.start)

    @pl.when(square != FAR + 1)
    def _():
        pass_on(1, 3)

    for copy in gathers:
        copy.wait_send()
    for turn in range(OWNERS):
        other, copy = to_owner(turn)
        pl.when(other)(copy.wait_send)

    @pl.when(is_owner)
    def _():
        for step in (1, 7, 2, 6, 3, 5, 4):
            source = lax.rem(square + step, SQUARES)
            if step in LAST:
                pl.when(square != 0)(functools.partial(wait_partial, source, held_strip))
            else:
                wait_partial(source, held_strip)
        added = partials[0, held_strip].astype(F32)
        for source in ORDER[1:]:
            added += partials[source, held_strip].astype(F32)
        total[...] = added

        @pl.when(square != 0)
        def _():
            added = total[...]
            for source in LAST:
                added += partials[source, held_strip].astype(F32)
            total[...] = added

        for turn in range(GROUP):
            other, copy = to_mate(turn)
            pl.when(other)(copy.start)

        @pl.when(own_table)
        def _():
            pltpu.make_async_copy(total, table.at[held_strip], table_recv.at[held_strip]).start()

    for strip in range(OWNERS):
        pltpu.make_async_copy(total, table.at[strip], table_recv.at[strip]).wait()

    @pl.when(is_owner)
    def _():
        for step in range(1, SQUARES):
            other, copy = across(step)
            pl.when(other)(copy.wait_send)
        for turn in range(GROUP):
            other, copy = to_mate(turn)
            pl.when(other)(copy.wait_send)

    @pl.when(square == 0)
    def _():
        added = table[...]
        for source in LAST:
            for strip in range(OWNERS):
                wait_partial(source, strip)
            added += partials[source].astype(F32)
        summed_ref[...] = added.reshape(KEPT, KEPT)

    @pl.when(square != 0)
    def _():
        summed_ref[...] = table[...].reshape(KEPT, KEPT)

    @pl.when(jnp.logical_and(is_far, is_owner))
    def _():
        for mate in range(GROUP):
            to_first(mate).wait_send()


def expand_kernel(summed_ref, wide, block_ref, out_hbm, out, out_sem):
    summed = two_parts(summed_ref[...], 0)
    half = fold_rows(dot(summed, wide[:KEPT])) + dot(summed[:KEPT], wide[KEPT:])
    half = two_parts(half, 0)
    square_basis = block_ref[...].astype(BF16)
    copies = []
    for i in range(4):
        high = half[32 * i : 32 * (i + 1)]
        low = half[KEPT + 32 * i : KEPT + 32 * (i + 1)]
        out[i] = dot(square_basis, jnp.concatenate([high, high, low], axis=0)).astype(BF16)
        copy = pltpu.make_async_copy(out.at[i], out_hbm.at[pl.ds(256 * i, 256)], out_sem.at[i])
        copy.start()
        copies.append(copy)
    for copy in copies:
        copy.wait()


def per_device(activations, output_gradient, momentum):
    wide = block_basis()
    corner = wide[:32, :256].T
    high = corner.astype(ml_dtypes.bfloat16).astype(np.float32)
    block = np.concatenate([high, corner - high, high], axis=1)
    wide, tall, block = jnp.asarray(wide), jnp.asarray(wide.T.copy()), jnp.asarray(block)
    anywhere = pl.BlockSpec(memory_space=pl.ANY)
    in_vmem = pl.BlockSpec(memory_space=pltpu.VMEM)
    dma = pltpu.SemaphoreType.DMA
    operands = (activations, output_gradient, momentum, wide, tall)
    summed, wide = pl.pallas_call(
        step_kernel,
        out_shape=(pltpu.VMEM((KEPT, KEPT), F32), pltpu.VMEM((2 * KEPT, ROWS), BF16)),
        in_specs=[anywhere] * 5,
        out_specs=(in_vmem, in_vmem),
        scratch_shapes=[
            pltpu.VMEM((TOKENS, ROWS), BF16),
            pltpu.VMEM((SHARE, COLS), BF16),
            pltpu.VMEM((ROWS, COLS), BF16),
            pltpu.VMEM((KEPT, ROWS), F32),
            pltpu.VMEM((ROWS, KEPT), F32),
            pltpu.VMEM((ROWS, 2 * KEPT), BF16),
            pltpu.VMEM((2 * KEPT, TOKENS), BF16),
            pltpu.VMEM((TOKENS, KEPT), BF16),
            pltpu.VMEM((OWNERS, STRIP, KEPT), BF16),
            pltpu.VMEM((GROUP, STRIP, KEPT), BF16),
            pltpu.VMEM((SQUARES, OWNERS, STRIP, KEPT), BF16),
            pltpu.VMEM((OWNERS, STRIP, KEPT), F32),
            pltpu.VMEM((STRIP, KEPT), F32),
            dma((8,)),
            dma((TENSOR,)),
            dma((TENSOR,)),
            dma((OWNERS,)),
            dma((GROUP,)),
            dma((GROUP,)),
            dma((SQUARES,)),
            dma((SQUARES, OWNERS)),
            dma((GROUP,)),
            dma((OWNERS,)),
            pltpu.SemaphoreType.REGULAR((2, 3)),
        ],
        compiler_params=pltpu.CompilerParams(
            collective_id=0, has_side_effects=True, vmem_limit_bytes=24 * 2**20
        ),
        name="step",
    )(*[pltpu.with_memory_space_constraint(value, pltpu.HBM) for value in operands])
    return pl.pallas_call(
        expand_kernel,
        out_shape=jax.ShapeDtypeStruct((ROWS, COLS), BF16),
        in_specs=[in_vmem] * 3,
        out_specs=anywhere,
        scratch_shapes=[pltpu.VMEM((4, 256, COLS), BF16), dma((4,))],
        compiler_params=pltpu.CompilerParams(vmem_limit_bytes=24 * 2**20),
        name="expand",
    )(summed, wide, block)


def solution(mesh):
    return jax.shard_map(
        per_device,
        mesh=mesh,
        in_specs=(P("dp", "tensor"), P(("dp", "tensor"), None), P("dp", "tensor", None)),
        out_specs=P("tensor", None),
        check_vma=False,
    )
```

```python
import functools

import jax
import jax.numpy as jnp
import numpy as np
from jax import lax
from jax.experimental import pallas as pl
from jax.experimental.pallas import tpu as pltpu
from jax.sharding import PartitionSpec as P
import ml_dtypes

BLOCK_SIDE = 64
KEPT_FREQUENCY = 8
MESH = pl.DeviceIdType.MESH
F32 = jnp.float32
BF16 = jnp.bfloat16

ROWS = 1024
COLS = 1024
TOKENS = 512
KEPT = ROWS // BLOCK_SIDE * KEPT_FREQUENCY
TENSOR = 8
SHARE = TOKENS // TENSOR
GROUP = 16
OWNERS = 8
STRIP = KEPT // OWNERS
SQUARES = 8
FAR = SQUARES // 2
ORDER = (0, 1, 2, 7, 6)
LAST = (3, 5, FAR)
LEVELS = (3, 3)


def block_basis():
    freq = np.arange(KEPT_FREQUENCY)[:, None]
    place = np.arange(BLOCK_SIDE)[None, :]
    scales = np.where(freq == 0, np.sqrt(1.0 / BLOCK_SIDE), np.sqrt(2.0 / BLOCK_SIDE))
    basis = scales * np.cos(np.pi * (2.0 * place + 1.0) * freq / (2.0 * BLOCK_SIDE))
    return np.kron(np.eye(ROWS // BLOCK_SIDE), basis).astype(np.float32)


def two_parts(value, axis):
    high = value.astype(BF16)
    low = (value - high.astype(F32)).astype(BF16)
    return jnp.concatenate([high, low], axis=axis)


def fold_rows(value):
    half = value.shape[0] // 2
    return value[:half] + value[half:]


def fold_cols(value):
    half = value.shape[1] // 2
    return value[:, :half] + value[:, half:]


def dot(a, b):
    return jnp.dot(a, b, preferred_element_type=F32)


def dot_nt(a, b):
    return lax.dot_general(a, b, (((1,), (1,)), ((), ())), preferred_element_type=F32)


def step_kernel(
    acts_hbm, grad_hbm, moment_hbm, wide_hbm, tall_hbm, summed_ref, wide,
    acts, grad, moment, wide_full, tall_full, tall, rows, gathered, coeffs, strips, partials, table, total,
    load_sem, gather_send, gather_recv, strip_send, strip_recv,
    first_send, across_send, partial_recv, table_send, table_recv, known,
):
    dp, tensor = lax.axis_index("dp"), lax.axis_index("tensor")
    square, place = dp // GROUP, lax.rem(dp, GROUP)
    core = lax.rem(tensor, 2)
    is_far = jnp.logical_and(square >= FAR - 1, square <= FAR + 1)

    is_owner = core == 1
    own_table = place >= OWNERS
    held = jnp.where(own_table, tensor, tensor - 1)
    held_strip = lax.rem(place, OWNERS)

    def peer(step):
        return (dp, lax.rem(tensor + step, TENSOR))

    def mate(step):
        return (square * GROUP + lax.rem(place + step, GROUP), tensor)

    def across_cores(step):
        return (square * GROUP + lax.rem(place + step, GROUP), tensor + 1 - 2 * core)

    def ahead(step):
        return (lax.rem(square + step, SQUARES) * GROUP + place, tensor)

    barrier = pltpu.get_barrier_semaphore()
    greeted = [ahead(1), ahead(SQUARES - 1)]
    greeted += [mate(step) for step in range(1, GROUP)]
    greeted += [across_cores(step) for step in range(1, GROUP)]
    greeted += [peer(step) for step in range(1, TENSOR)]
    for device in greeted:
        pl.semaphore_signal(barrier, inc=1, device_id=device, device_id_type=MESH)

    @pl.when(square == 0)
    def _():
        for step in range(GROUP):
            spot = GROUP + lax.rem(place + step, GROUP)
            for other in (tensor, tensor + 1 - 2 * core)[1 if step == 0 else 0 :]:
                pl.semaphore_signal(
                    barrier, inc=1, device_id=(spot, other), device_id_type=MESH
                )

    loads = [
        pltpu.make_async_copy(source, target, load_sem.at[i])
        for i, (source, target) in enumerate(
            [(grad_hbm, grad), (tall_hbm, tall_full), (wide_hbm, wide_full), (acts_hbm, acts)]
            + [
                (moment_hbm.at[0, pl.ds(256 * i, 256)], moment.at[pl.ds(256 * i, 256)])
                for i in range(4)
            ]
        )
    ]
    for load in loads:
        load.start()

    loads[0].wait()
    loads[1].wait()
    tall[...] = two_parts(tall_full[...], 1)
    mine = pl.ds(pl.multiple_of(tensor * SHARE, SHARE), SHARE)
    gathered[mine] = fold_cols(dot(grad[...], tall[...])).astype(BF16)
    pl.semaphore_wait(barrier, len(greeted) + jnp.where(square == 1, 2 * GROUP - 1, 0))
    gathers = []
    for step in (4, 5 - 2 * core, 3 + 2 * core, 2, 6, 7, 1):
        copy = pltpu.make_async_remote_copy(
            src_ref=gathered.at[mine],
            dst_ref=gathered.at[mine],
            send_sem=gather_send.at[step],
            recv_sem=gather_recv.at[step],
            device_id=peer(step),
            device_id_type=MESH,
        )
        copy.start()
        gathers.append(copy)

    def pass_on(way, level):
        if level > 0:
            pl.semaphore_wait(known.at[way, level - 1], 1)
        if level < LEVELS[way]:
            target = ahead(1) if way == 0 else ahead(SQUARES - 1)
            pl.semaphore_signal(known.at[way, level], inc=1, device_id=target, device_id_type=MESH)

    pass_on(0, 0)
    pass_on(1, 0)

    loads[2].wait()
    wide[...] = two_parts(wide_full[...], 0)
    loads[3].wait()
    rows[...] = two_parts(fold_rows(dot_nt(wide[...], acts[...])), 0)
    kept = jnp.zeros((2 * KEPT, 2 * KEPT), F32)
    for i in range(4):
        loads[4 + i].wait()
        part = slice(256 * i, 256 * (i + 1))
        half = two_parts(fold_cols(dot(moment[part], tall[...])), 1)
        kept += dot(wide[:, part], half)
    kept = 0.9 * fold_cols(fold_rows(kept))

    pass_on(0, 1)
    pass_on(1, 1)

    def of_chip(step):
        spot = lax.rem(tensor // 2 + step, TENSOR // 2) * 2 * SHARE
        tokens = pl.ds(pl.multiple_of(spot, 2 * SHARE), 2 * SHARE)
        return dot(rows[:, tokens], gathered[tokens])

    def wait_tokens(step):
        pltpu.make_async_copy(gathered.at[mine], gathered.at[mine], gather_recv.at[step]).wait()

    for step in (1, 2, 6, 7, 5 - 2 * core):
        wait_tokens(step)
    found = of_chip(0) + of_chip(1) + of_chip(3)
    for step in (4, 3 + 2 * core):
        wait_tokens(step)
    found = fold_rows(found + of_chip(2)) + kept
    coeffs[...] = found.reshape(OWNERS, STRIP, KEPT).astype(BF16)

    def to_owner(turn):
        strip = 4 * (turn % 2) + lax.rem(place + (2, 1, 3, 0)[turn // 2], 4)
        owner = strip + OWNERS * core
        return jnp.logical_or(core == 0, owner != place), pltpu.make_async_remote_copy(
            src_ref=coeffs.at[strip],
            dst_ref=strips.at[place],
            send_sem=strip_send.at[turn],
            recv_sem=strip_recv.at[place],
            device_id=(square * GROUP + owner, tensor + 1 - core),
            device_id_type=MESH,
        )

    for turn in range(OWNERS):
        other, copy = to_owner(turn)
        pl.when(other)(copy.start)
    pass_on(0, 2)
    pass_on(1, 2)
    pass_on(0, 3)

    def to_first(mate):
        return pltpu.make_async_remote_copy(
            src_ref=partials.at[square, held_strip],
            dst_ref=partials.at[square, held_strip],
            send_sem=first_send.at[mate],
            recv_sem=partial_recv.at[square, held_strip],
            device_id=(mate, held),
            device_id_type=MESH,
        )

    def across(step):
        return jnp.logical_or(jnp.logical_not(is_far), square + step != SQUARES), pltpu.make_async_remote_copy(
            src_ref=partials.at[square, held_strip],
            dst_ref=partials.at[square, held_strip],
            send_sem=across_send.at[step],
            recv_sem=partial_recv.at[square, held_strip],
            device_id=ahead(step),
            device_id_type=MESH,
        )

    def to_mate(turn):
        mate = turn // 4 * 4 + lax.rem(place + (2, 1, 3, 0)[turn % 4], 4)
        elsewhere = jnp.logical_or(jnp.logical_not(own_table), mate != place)
        return elsewhere, pltpu.make_async_remote_copy(
            src_ref=total,
            dst_ref=table.at[held_strip],
            send_sem=table_send.at[turn],
            recv_sem=table_recv.at[held_strip],
            device_id=(square * GROUP + mate, held),
            device_id_type=MESH,
        )

    def wait_strip(source):
        pltpu.make_async_copy(strips.at[source], strips.at[source], strip_recv.at[source]).wait()

    def wait_partial(source, strip):
        piece = partials.at[source, strip]
        pltpu.make_async_copy(piece, piece, partial_recv.at[source, strip]).wait()

    @pl.when(is_owner)
    def _():
        for step in range(1, GROUP):
            wait_strip(lax.rem(place + step, GROUP))

        @pl.when(own_table)
        def _():
            strips[place] = coeffs[held_strip]

        pl.when(jnp.logical_not(own_table))(functools.partial(wait_strip, place))
        partials[square, held_strip] = jnp.sum(strips[...].astype(F32), axis=0).astype(BF16)

    @pl.when(square == FAR + 1)
    def _():
        pass_on(1, 3)

    @pl.when(jnp.logical_and(is_far, is_owner))
    def _():
        for mate in range(GROUP):
            to_first(mate).start()

    @pl.when(is_owner)
    def _():
        for step in (4, 3, 5, 2, 6, 1, 7):
            other, copy = across(step)
            pl.when(other)(copy.start)

    @pl.when(square != FAR + 1)
    def _():
        pass_on(1, 3)

    for copy in gathers:
        copy.wait_send()
    for turn in range(OWNERS):
        other, copy = to_owner(turn)
        pl.when(other)(copy.wait_send)

    @pl.when(is_owner)
    def _():
        for step in (1, 7, 2, 6, 3, 5, 4):
            source = lax.rem(square + step, SQUARES)
            if step in LAST:
                pl.when(square != 0)(functools.partial(wait_partial, source, held_strip))
            else:
                wait_partial(source, held_strip)
        added = partials[0, held_strip].astype(F32)
        for source in ORDER[1:]:
            added += partials[source, held_strip].astype(F32)
        total[...] = added

        @pl.when(square != 0)
        def _():
            added = total[...]
            for source in LAST:
                added += partials[source, held_strip].astype(F32)
            total[...] = added

        for turn in range(GROUP):
            other, copy = to_mate(turn)
            pl.when(other)(copy.start)

        @pl.when(own_table)
        def _():
            pltpu.make_async_copy(total, table.at[held_strip], table_recv.at[held_strip]).start()

    for strip in range(OWNERS):
        pltpu.make_async_copy(total, table.at[strip], table_recv.at[strip]).wait()

    @pl.when(is_owner)
    def _():
        for step in range(1, SQUARES):
            other, copy = across(step)
            pl.when(other)(copy.wait_send)
        for turn in range(GROUP):
            other, copy = to_mate(turn)
            pl.when(other)(copy.wait_send)

    @pl.when(square == 0)
    def _():
        added = table[...]
        for source in LAST:
            for strip in range(OWNERS):
                wait_partial(source, strip)
            added += partials[source].astype(F32)
        summed_ref[...] = added.reshape(KEPT, KEPT)

    @pl.when(square != 0)
    def _():
        summed_ref[...] = table[...].reshape(KEPT, KEPT)

    @pl.when(jnp.logical_and(is_far, is_owner))
    def _():
        for mate in range(GROUP):
            to_first(mate).wait_send()


def expand_kernel(summed_ref, wide, block_ref, out_hbm, out, out_sem):
    summed = two_parts(summed_ref[...], 0)
    half = fold_rows(dot(summed, wide[:KEPT])) + dot(summed[:KEPT], wide[KEPT:])
    half = two_parts(half, 0)
    square_basis = block_ref[...].astype(BF16)
    copies = []
    for i in range(8):
        high = half[16 * i : 16 * (i + 1)]
        low = half[KEPT + 16 * i : KEPT + 16 * (i + 1)]
        out[i] = dot(square_basis, jnp.concatenate([high, high, low], axis=0)).astype(BF16)
        copy = pltpu.make_async_copy(out.at[i], out_hbm.at[pl.ds(128 * i, 128)], out_sem.at[i])
        copy.start()
        copies.append(copy)
    for copy in copies:
        copy.wait()


def per_device(activations, output_gradient, momentum):
    wide = block_basis()
    corner = wide[:16, :128].T
    high = corner.astype(ml_dtypes.bfloat16).astype(np.float32)
    block = np.concatenate([high, corner - high, high], axis=1)
    wide, tall, block = jnp.asarray(wide), jnp.asarray(wide.T.copy()), jnp.asarray(block)
    anywhere = pl.BlockSpec(memory_space=pl.ANY)
    in_vmem = pl.BlockSpec(memory_space=pltpu.VMEM)
    dma = pltpu.SemaphoreType.DMA
    operands = (activations, output_gradient, momentum, wide, tall)
    summed, wide = pl.pallas_call(
        step_kernel,
        out_shape=(pltpu.VMEM((KEPT, KEPT), F32), pltpu.VMEM((2 * KEPT, ROWS), BF16)),
        in_specs=[anywhere] * 5,
        out_specs=(in_vmem, in_vmem),
        scratch_shapes=[
            pltpu.VMEM((TOKENS, ROWS), BF16),
            pltpu.VMEM((SHARE, COLS), BF16),
            pltpu.VMEM((ROWS, COLS), BF16),
            pltpu.VMEM((KEPT, ROWS), F32),
            pltpu.VMEM((ROWS, KEPT), F32),
            pltpu.VMEM((ROWS, 2 * KEPT), BF16),
            pltpu.VMEM((2 * KEPT, TOKENS), BF16),
            pltpu.VMEM((TOKENS, KEPT), BF16),
            pltpu.VMEM((OWNERS, STRIP, KEPT), BF16),
            pltpu.VMEM((GROUP, STRIP, KEPT), BF16),
            pltpu.VMEM((SQUARES, OWNERS, STRIP, KEPT), BF16),
            pltpu.VMEM((OWNERS, STRIP, KEPT), F32),
            pltpu.VMEM((STRIP, KEPT), F32),
            dma((8,)),
            dma((TENSOR,)),
            dma((TENSOR,)),
            dma((OWNERS,)),
            dma((GROUP,)),
            dma((GROUP,)),
            dma((SQUARES,)),
            dma((SQUARES, OWNERS)),
            dma((GROUP,)),
            dma((OWNERS,)),
            pltpu.SemaphoreType.REGULAR((2, 3)),
        ],
        compiler_params=pltpu.CompilerParams(
            collective_id=0, has_side_effects=True, vmem_limit_bytes=24 * 2**20
        ),
        name="step",
    )(*[pltpu.with_memory_space_constraint(value, pltpu.HBM) for value in operands])
    return pl.pallas_call(
        expand_kernel,
        out_shape=jax.ShapeDtypeStruct((ROWS, COLS), BF16),
        in_specs=[in_vmem] * 3,
        out_specs=anywhere,
        scratch_shapes=[pltpu.VMEM((8, 128, COLS), BF16), dma((8,))],
        compiler_params=pltpu.CompilerParams(vmem_limit_bytes=24 * 2**20),
        name="expand",
    )(summed, wide, block)


def solution(mesh):
    return jax.shard_map(
        per_device,
        mesh=mesh,
        in_specs=(P("dp", "tensor"), P(("dp", "tensor"), None), P("dp", "tensor", None)),
        out_specs=P("tensor", None),
        check_vma=False,
    )
```
